32 devices in a mesh: leaf: 2 (over x), grid: 16 (over z, y, core).
Axes of the slice: x: 2, y: 2, z: 4, core: 2. Of those that a mesh axis runs over, the one named last changes fastest.
Arguments:
- front_diag: float32 [2, 8192], P('leaf', 'grid'), may hold values from 1 to 4
- children: bfloat16 [4, 4096, 4096], P('leaf', 'grid'), may hold values from 0 to 1, as said below
- parent: int32 [4], replicated, may hold values from 0 to 1, as said below
- front_blocks: int32 [2], replicated, may hold values from 64 to 128
- child_blocks: int32 [4], replicated, may hold values from 32 to 64
- row_map: int32 [4, 64], replicated, may hold values from 0 to 127, as said below
Outputs:
- factor: bfloat16 [2, 8192, 8192], P('leaf', 'grid')
The draws below stay inside these ranges and needn't reach their ends.
Inputs may be any that keep to these rules, and one draw needn't show every extreme that they name: Children 2 l and 2 l + 1 belong to leaf index l; one of them has parent l and the other has parent l xor 1, so each front has exactly two children. Each row_map[c] holds 64 distinct increasing block numbers, all below front_blocks[parent[c]]; only its first child_blocks[c] entries are used. Each children[c] is symmetric.
All inputs are finite; a program needn't handle non-finite values.
Results may differ from the reference program's by a relative error of at most 0.003.
The reference program's roundings to bfloat16 on the way count: a program that leaves them out, or rounds other values in their place, can miss the bound.
Values may be sent and summed in bfloat16 or wider, within the bound.
A program may use at most 128 MiB of HBM per device.

```python
import math
import jax
import jax.numpy as jnp
from jax import lax

F = 8192
CU = 4096
BLK = 64
PW = 256
PANELS = 3
FRONTS = 2
CHILDREN = 4
FRONT_BLOCKS = 128
CHILD_BLOCKS = 64


def shuffled(subkey):
    return jax.random.permutation(subkey, FRONT_BLOCKS)


def tree_tables(key):
    bits = jax.random.randint(jax.random.fold_in(key, 101), (FRONTS,), 0, 2)
    child_index = jnp.arange(CHILDREN, dtype=jnp.int32)
    home = child_index // 2
    parent = jnp.where(child_index % 2 == bits[home], home, jnp.bitwise_xor(home, 1)).astype(jnp.int32)
    front_blocks = jax.random.randint(jax.random.fold_in(key, 102), (FRONTS,), FRONT_BLOCKS // 2, FRONT_BLOCKS + 1)
    order = jax.random.permutation(jax.random.fold_in(key, 103), FRONTS)
    front_blocks = front_blocks.at[order[0]].set(FRONT_BLOCKS).at[order[1]].set(FRONT_BLOCKS // 2)
    child_blocks = jax.random.randint(jax.random.fold_in(key, 104), (CHILDREN,), CHILD_BLOCKS // 2, CHILD_BLOCKS + 1)
    second = jax.random.permutation(jax.random.fold_in(key, 105), CHILDREN)
    child_blocks = child_blocks.at[second[0]].set(CHILD_BLOCKS).at[second[1]].set(CHILD_BLOCKS // 2)
    subkeys = jax.random.split(jax.random.fold_in(key, 106), CHILDREN)
    scores = jax.vmap(shuffled)(subkeys)
    limit = front_blocks[parent][:, None]
    places = jnp.arange(FRONT_BLOCKS, dtype=jnp.int32)[None, :]
    ranked = jnp.where(places < limit, scores, FRONT_BLOCKS + places)
    forced = (places == 0) | (places == limit - 1)
    ranked = jnp.where(forced, -1, ranked)
    chosen = jnp.argsort(ranked, axis=1, stable=True)[:, :CHILD_BLOCKS]
    row_map = jnp.sort(chosen, axis=1).astype(jnp.int32)
    return (parent, front_blocks.astype(jnp.int32), child_blocks.astype(jnp.int32), row_map)


def draw_parent(key, part):
    return tree_tables(key)[0]


def draw_front_blocks(key, part):
    return tree_tables(key)[1]


def draw_child_blocks(key, part):
    return tree_tables(key)[2]


def draw_row_map(key, part):
    return tree_tables(key)[3]


def draw_children(key, part):
    reach = 0.6

    def kernel_child(child_key):
        coords = jax.random.uniform(child_key, (3, CU), jnp.float32)
        distance = jnp.zeros((CU, CU), jnp.float32)
        for direction in range(3):
            distance = distance + jnp.abs(coords[direction][:, None] - coords[direction][None, :])
        return jnp.exp(-distance / reach)
    child_keys = jax.random.split(jax.random.fold_in(key, 201), CHILDREN)
    return lax.map(kernel_child, child_keys).astype(jnp.bfloat16)


def levels(rng, extent, pieces, smallest, high):
    def one(dim, blocks):
        steps = jax.random.uniform(jax.random.fold_in(jax.random.fold_in(rng, 6), dim), (blocks,), jnp.float32, smallest / len(pieces), high / len(pieces))
        return jnp.repeat(jnp.exp(steps), extent[dim] // blocks).reshape((-1,) + (1,) * (len(extent) - dim - 1))

    factor_of = one(*pieces[0])
    for cut in pieces[1:]:
        factor_of = factor_of * one(*cut)
    return factor_of


def setup_inputs(seed: int = 0) -> dict:
    key_list = jax.random.split(jax.random.key(seed), 7)
    front_diag = jnp.clip(jnp.exp(math.log(4.0) - 1.3862944 * jax.random.uniform(key_list[0], (FRONTS, F), jnp.float32) ** levels(key_list[0], (FRONTS, F), ((0, 2), (1, 16)), -0.2, 0.2)), 1.0, 4.0)
    children = draw_children(jax.random.fold_in(key_list[6], 71), 0)
    parent = draw_parent(jax.random.fold_in(key_list[6], 71), 0)
    front_blocks = draw_front_blocks(jax.random.fold_in(key_list[6], 71), 0)
    child_blocks = draw_child_blocks(jax.random.fold_in(key_list[6], 71), 0)
    row_map = draw_row_map(jax.random.fold_in(key_list[6], 71), 0)
    return {"front_diag": front_diag, "children": children, "parent": parent, "front_blocks": front_blocks, "child_blocks": child_blocks, "row_map": row_map}


def pivot_parts(pivot_block):
    pivot_factor = jnp.linalg.cholesky(pivot_block)
    identity = jnp.eye(pivot_block.shape[0], dtype=pivot_block.dtype)
    pivot_inverse = jax.scipy.linalg.solve_triangular(pivot_factor, identity, lower=True)
    return (pivot_factor, pivot_inverse)

def assemble(front_index, front_diag, children, parent, front_blocks, child_blocks, row_map):
    matrix = jnp.zeros((F, F), jnp.float32)
    child_ids = jnp.nonzero(parent == front_index, size=2)[0]
    for slot in range(2):
        child_index = child_ids[slot]
        update_block = children[child_index].astype(jnp.float32)
        live = (jnp.arange(CU) // BLK < child_blocks[child_index]).astype(jnp.float32)
        update_block = update_block * live[:, None] * live[None, :]
        positions = (row_map[child_index][:, None] * BLK + jnp.arange(BLK)[None, :]).reshape(-1)
        matrix = matrix.at[positions[:, None], positions[None, :]].add(update_block)
    line = jnp.arange(F)
    active = front_blocks[front_index] * BLK
    on_diag = line[:, None] == line[None, :]
    matrix = matrix + jnp.where(on_diag, front_diag[front_index][:, None], jnp.float32(0.0))
    padding = (line[:, None] >= active) | (line[None, :] >= active)
    identity_part = jnp.where(on_diag, jnp.float32(1.0), jnp.float32(0.0))
    matrix = jnp.where(padding, identity_part, matrix)
    return matrix.astype(jnp.bfloat16)

def factor_front(matrix):
    for step in range(PANELS):
        left_edge = step * PW
        right_edge = left_edge + PW
        pivot_block = matrix[left_edge:right_edge, left_edge:right_edge].astype(jnp.float32)
        pivot_factor, pivot_inverse = pivot_parts(pivot_block)
        below = jnp.dot(matrix[right_edge:, left_edge:right_edge].astype(jnp.float32), pivot_inverse.T, precision=lax.Precision.HIGHEST)
        upper_zero = jnp.zeros((left_edge, PW), jnp.float32)
        panel_cols = jnp.concatenate([upper_zero, pivot_factor, below], 0).astype(jnp.bfloat16)
        lower_panel = panel_cols[right_edge:]
        trailing = matrix[right_edge:, right_edge:].astype(jnp.float32) - jnp.dot(lower_panel.astype(jnp.float32), lower_panel.T.astype(jnp.float32), preferred_element_type=jnp.float32)
        matrix = matrix.at[right_edge:, right_edge:].set(trailing.astype(jnp.bfloat16))
        matrix = matrix.at[:right_edge, right_edge:].set(jnp.zeros((right_edge, F - right_edge), jnp.bfloat16))
        matrix = matrix.at[:, left_edge:right_edge].set(panel_cols)
    return matrix

def reference(front_diag, children, parent, front_blocks, child_blocks, row_map):

    def one_front(front_index):
        assembled = assemble(front_index, front_diag, children, parent, front_blocks, child_blocks, row_map)
        return factor_front(assembled)
    return lax.map(one_front, jnp.arange(FRONTS, dtype=jnp.int32))
```

```python
import functools
import jax
import jax.numpy as jnp
from jax import lax
from jax.experimental import pallas as pl
from jax.experimental.pallas import tpu as pltpu
from jax.sharding import PartitionSpec as P

BLK = 64
PW = 256
PANELS = 3
TOP = PW * PANELS
UNIT = PW // BLK
F32 = jnp.float32
BF16 = jnp.bfloat16
VMEM_LIMIT = 56 * 1024 * 1024


def swapped(value, axis, distance):
    mask = 2**distance
    pairs = [(source, source ^ mask) for source in range(lax.axis_size(axis))]
    return lax.ppermute(value, axis, pairs)


def pivot_parts(pivot_block):
    pivot_factor = jnp.linalg.cholesky(pivot_block)
    identity = jnp.eye(PW, dtype=F32)
    pivot_inverse = jax.scipy.linalg.solve_triangular(pivot_factor, identity, lower=True)
    return (pivot_factor, pivot_inverse)


def split3(value):
    hi = value.astype(BF16)
    rest = value - hi.astype(F32)
    mid = rest.astype(BF16)
    return hi, mid, (rest - mid.astype(F32)).astype(BF16)


def dot_nt(a, b):
    return lax.dot_general(a, b, (((1,), (1,)), ((), ())), preferred_element_type=F32)


def spread_kernel(lane_start, src_ref, child_ref, out_ref, *, window):
    start = pl.multiple_of(lane_start[pl.program_id(0)] * 128, 128)
    ids = lax.broadcasted_iota(jnp.int32, (window, src_ref.shape[1]), 0)
    pick = (ids == src_ref[...] - start).astype(F32).astype(BF16)
    values = child_ref[:, pl.ds(start, window)]
    out_ref[0] = jnp.dot(values, pick, preferred_element_type=F32).astype(BF16)


def spread(child, lane_start, source_cols, grid_size, window):
    child_rows, child_order = child.shape
    rows_here = source_cols.shape[1] // grid_size
    return pl.pallas_call(
        functools.partial(spread_kernel, window=window),
        grid_spec=pltpu.PrefetchScalarGridSpec(
            num_scalar_prefetch=1,
            grid=(grid_size,),
            in_specs=[
                pl.BlockSpec((1, rows_here), lambda t, s: (0, t)),
                pl.BlockSpec((child_rows, child_order), lambda t, s: (0, 0)),
            ],
            out_specs=pl.BlockSpec((1, child_rows, rows_here), lambda t, s: (t, 0, 0)),
        ),
        out_shape=jax.ShapeDtypeStruct((grid_size, child_rows, rows_here), BF16),
        compiler_params=pltpu.CompilerParams(vmem_limit_bytes=VMEM_LIMIT),
        cost_estimate=pl.CostEstimate(
            flops=2 * child_rows * window * source_cols.shape[1],
            bytes_accessed=6 * child_rows * source_cols.shape[1],
            transcendentals=0,
        ),
    )(lane_start, source_cols, child)


def panels_kernel(inverse, c0, c1, c2, place, factors, solves, crosses, out_ref, parts):
    tile = pl.program_id(0)
    blocks = inverse.shape[0] // 2

    @pl.when(tile == 0)
    def _():
        for step in range(PANELS):
            for index, part in enumerate(split3(solves[step])):
                parts[step, index] = part

    rows = []
    for child in range(2):
        picked = []
        for chunk in (c0, c1, c2):
            pieces = []
            for unit in range(UNIT):
                block = inverse[child * blocks + tile * UNIT + unit]
                at = pl.multiple_of(jnp.maximum(block, 0) * BLK, BLK)
                piece = chunk[pl.ds(at, BLK), child * PW : (child + 1) * PW].astype(F32)
                pieces.append(jnp.where(block >= 0, piece, 0.0).astype(BF16))
            picked.append(jnp.concatenate(pieces, axis=0))
        rows.append(picked)
    done = []
    for step in range(PANELS):
        low, high = step * PW, (step + 1) * PW
        total = jnp.zeros((PW, PW), F32)
        for child in range(2):
            for chunk in range(step + 1):
                total += jnp.dot(
                    rows[child][chunk],
                    place[child, chunk * PW : (chunk + 1) * PW, low:high],
                    preferred_element_type=F32,
                )
        current = total.astype(BF16)
        for earlier in range(step):
            cross = crosses[low:high, earlier * PW : (earlier + 1) * PW]
            current = (current.astype(F32) - dot_nt(done[earlier], cross)).astype(BF16)
        solved = dot_nt(current, parts[step, 2]) + dot_nt(current, parts[step, 1])
        solved = solved + dot_nt(current, parts[step, 0])
        chosen = jnp.where(tile == step, factors[step], solved)
        chosen = jnp.where(tile < step, 0.0, chosen).astype(BF16)
        done.append(chosen)
        out_ref[:, low:high] = chosen


def panels(inverse, chunks, place, factors, solves, crosses, front_order):
    whole = lambda shape: pl.BlockSpec(shape, lambda t, s: (0,) * len(shape))
    return pl.pallas_call(
        panels_kernel,
        grid_spec=pltpu.PrefetchScalarGridSpec(
            num_scalar_prefetch=1,
            grid=(front_order // PW,),
            in_specs=[whole(x.shape) for x in (*chunks, place, factors, solves, crosses)],
            out_specs=pl.BlockSpec((PW, TOP), lambda t, s: (t, 0)),
            scratch_shapes=[pltpu.VMEM((PANELS, 3, PW, PW), BF16)],
        ),
        out_shape=jax.ShapeDtypeStruct((front_order, TOP), BF16),
        compiler_params=pltpu.CompilerParams(vmem_limit_bytes=VMEM_LIMIT),
    )(inverse, *chunks, place, factors, solves, crosses)


def trailing_kernel(scalars, src_ref, diag_ref, own_ref, far_ref, mine_ref, tile_ref, out_ref):
    tile = pl.program_id(0)
    rows_here = out_ref.shape[0]
    tiles = pl.num_programs(0)
    active, first_row = scalars[2 * tiles], scalars[2 * tiles + 1]

    @pl.when(tile < PANELS)
    def _():
        for step in range(PANELS):
            @pl.when(tile == step)
            def _():
                out_ref[...] = mine_ref[:, step * PW : (step + 1) * PW]

    @pl.when(tile >= PANELS)
    def _():
        ids = lax.broadcasted_iota(jnp.int32, (PW, PW), 0)
        total = None
        for child, ref in enumerate((own_ref, far_ref)):
            start = pl.multiple_of(scalars[child * tiles + tile] * BLK, BLK)
            pick = (ids == src_ref[child : child + 1, :] - start).astype(F32).astype(BF16)
            term = lax.dot_general(
                ref[pl.ds(start, PW), :], pick, (((0,), (0,)), ((), ())),
                preferred_element_type=F32,
            )
            total = term if total is None else total + term
        row = first_row + lax.broadcasted_iota(jnp.int32, (rows_here, PW), 0)
        col = tile * PW + lax.broadcasted_iota(jnp.int32, (rows_here, PW), 1)
        on_diag = row == col
        total = total + jnp.where(on_diag, diag_ref[...], 0.0)
        padding = (row >= active) | (col >= active)
        current = jnp.where(padding, jnp.where(on_diag, 1.0, 0.0), total).astype(BF16)
        for step in range(PANELS):
            low, high = step * PW, (step + 1) * PW
            product = dot_nt(mine_ref[:, low:high], tile_ref[:, low:high])
            current = (current.astype(F32) - product).astype(BF16)
        out_ref[...] = jnp.where(row < TOP, 0.0, current.astype(F32)).astype(BF16)


def trailing(scalars, source_rows, diag, own, far, mine, factor):
    front_order = factor.shape[0]
    rows_here = mine.shape[0]
    tiles = front_order // PW
    whole = lambda x: pl.BlockSpec(x.shape, lambda t, s: (0,) * x.ndim)
    return pl.pallas_call(
        trailing_kernel,
        grid_spec=pltpu.PrefetchScalarGridSpec(
            num_scalar_prefetch=1,
            grid=(tiles,),
            in_specs=[
                pl.BlockSpec((2, PW), lambda t, s: (0, t)),
                whole(diag), whole(own), whole(far), whole(mine),
                pl.BlockSpec((PW, TOP), lambda t, s: (t, 0)),
            ],
            out_specs=pl.BlockSpec((rows_here, PW), lambda t, s: (0, t)),
        ),
        out_shape=jax.ShapeDtypeStruct((rows_here, front_order), BF16),
        compiler_params=pltpu.CompilerParams(vmem_limit_bytes=VMEM_LIMIT),
    )(scalars, source_rows, diag, own, far, mine, factor)


def highest(a, b):
    return jnp.dot(a.astype(F32), b, precision=lax.Precision.HIGHEST)


def pivot_chain(tops):
    factors, inverses, rows_of = [], [], []
    for step in range(PANELS):
        low = step * PW
        current = tops[step][low:]
        for earlier in range(step):
            lower = rows_of[earlier][low:]
            product = dot_nt(lower, lower[:PW])
            current = (current.astype(F32) - product).astype(BF16)
        factor, inverse = pivot_parts(current[:PW].astype(F32))
        factors.append(factor)
        inverses.append(inverse)
        below = highest(current[PW:], inverse.T).astype(BF16)
        head = jnp.zeros((low + PW, PW), BF16)
        rows_of.append(jnp.concatenate([head, below], axis=0))
    return jnp.stack(factors), jnp.stack(inverses), jnp.concatenate(rows_of, axis=1)


def body(front_diag, children, parent, front_blocks, child_blocks, row_map):
    leaf_id = lax.axis_index("leaf")
    grid_id = lax.axis_index("grid")
    grid_size = lax.axis_size("grid")
    rows_here = front_diag.shape[1]
    front_order = rows_here * grid_size
    child_order = children.shape[2]
    blocks_front = front_order // BLK
    blocks_child = child_order // BLK
    partner = jnp.bitwise_xor(leaf_id, 1)
    first_child = 2 * leaf_id
    keep_first = parent[first_child] == leaf_id
    own_child = jnp.where(keep_first, first_child, first_child + 1)
    partner_first = 2 * partner
    far_child = jnp.where(parent[partner_first] == leaf_id, partner_first, partner_first + 1)
    own_part = jnp.where(keep_first, children[0], children[1])
    away_part = jnp.where(keep_first, children[1], children[0])

    strip_far = swapped(away_part[:, :TOP], "leaf", 0)
    arrived = swapped(away_part, "leaf", 0)
    diag_all = lax.all_gather(front_diag[0], "grid", axis=0, tiled=True)
    chunks = []
    for step in range(PANELS):
        low, high = step * PW, (step + 1) * PW
        pair = jnp.concatenate([own_part[:, low:high], strip_far[:, low:high]], axis=1)
        chunks.append(lax.all_gather(pair, "grid", axis=0, tiled=True))

    ids = jnp.stack([own_child, far_child])
    maps = row_map[ids]
    live = jnp.arange(blocks_child)[None, :] < child_blocks[ids][:, None]
    hits = (maps[:, :, None] == jnp.arange(blocks_front)[None, None, :]) & live[:, :, None]
    inverse = jnp.max(jnp.where(hits, jnp.arange(blocks_child)[None, :, None], -1), axis=1)
    source = jnp.where(
        inverse[:, :, None] >= 0, inverse[:, :, None] * BLK + jnp.arange(BLK), -(2**20)
    ).reshape(2, front_order).astype(jnp.int32)
    filled = (inverse >= 0).astype(jnp.int32)
    before = jnp.cumsum(filled, axis=1) - filled
    per_device = rows_here // BLK
    window = (per_device + 2) * BLK
    lane_start = jnp.minimum(before[:, ::per_device] // 2, (child_order - window) // 128)
    row_start = jnp.minimum(before[:, ::UNIT], blocks_child - UNIT)

    own_spread = spread(own_part, lane_start[0], source[0:1], grid_size, window)
    own_rows = lax.all_to_all(own_spread, "grid", split_axis=0, concat_axis=0, tiled=True)
    far_spread = spread(arrived, lane_start[1], source[1:2], grid_size, window)
    far_rows = lax.all_to_all(far_spread, "grid", split_axis=0, concat_axis=0, tiled=True)

    place = (jnp.arange(TOP)[None, :, None] == source[:, None, :TOP]).astype(BF16)
    tops = []
    for step in range(PANELS):
        low, high = step * PW, (step + 1) * PW
        total = jnp.zeros((TOP, PW), F32)
        for child in range(2):
            part = jnp.zeros((TOP, PW), F32)
            for chunk in range(step + 1):
                rows = chunks[chunk][:TOP, child * PW : (child + 1) * PW]
                part = part + jnp.dot(
                    rows, place[child, chunk * PW : (chunk + 1) * PW, low:high],
                    preferred_element_type=F32,
                )
            total = total + lax.dot_general(
                place[child], part.astype(BF16), (((0,), (0,)), ((), ())),
                preferred_element_type=F32,
            )
        shifted = jnp.arange(TOP)[:, None] == jnp.arange(low, high)[None, :]
        total = total + jnp.where(shifted, diag_all[:TOP, None], 0.0)
        tops.append(total.astype(BF16))
    factors, inverses, crosses = pivot_chain(tops)
    factor = panels(
        inverse.reshape(-1).astype(jnp.int32), chunks, place, factors, inverses, crosses, front_order
    )
    mine = lax.dynamic_slice_in_dim(factor, grid_id * rows_here, rows_here, axis=0)
    scalars = jnp.concatenate(
        [row_start.reshape(-1), (front_blocks[leaf_id] * BLK)[None], (grid_id * rows_here)[None]]
    ).astype(jnp.int32)
    matrix = trailing(
        scalars, source, front_diag[0][:, None],
        own_rows.reshape(child_order, rows_here), far_rows.reshape(child_order, rows_here),
        mine, factor,
    )
    return matrix[None]


def solution(mesh):
    in_specs = (P("leaf", "grid"), P("leaf", "grid", None), P(), P(), P(), P())
    out_specs = P("leaf", "grid", None)
    return jax.shard_map(body, mesh=mesh, in_specs=in_specs, out_specs=out_specs, check_vma=False)
```

```python
import functools
import jax
import jax.numpy as jnp
from jax import lax
from jax.experimental import pallas as pl
from jax.experimental.pallas import tpu as pltpu
from jax.sharding import PartitionSpec as P

BLK = 64
PW = 256
PANELS = 3
TOP = PW * PANELS
UNIT = PW // BLK
TILE = 512
EXTRA = 16
F32 = jnp.float32
BF16 = jnp.bfloat16
VMEM_LIMIT = 56 * 1024 * 1024


def swapped(value, axis, distance):
    mask = 2**distance
    pairs = [(source, source ^ mask) for source in range(lax.axis_size(axis))]
    return lax.ppermute(value, axis, pairs)


def highest(a, b):
    return jnp.dot(a.astype(F32), b, precision=lax.Precision.HIGHEST)


def rounded(value):
    return lax.reduce_precision(value, 8, 7)


def triangular_parts(block):
    factor = jnp.linalg.cholesky(block, symmetrize_input=False)
    identity = jnp.eye(block.shape[0], dtype=F32)
    return factor, jax.scipy.linalg.solve_triangular(factor, identity, lower=True)


def pivot_parts(pivot_block):
    half = PW // 2
    first, first_inverse = triangular_parts(pivot_block[:half, :half])
    cross = highest(pivot_block[half:, :half], first_inverse.T)
    second, second_inverse = triangular_parts(pivot_block[half:, half:] - highest(cross, cross.T))
    cross_inverse = -highest(second_inverse, highest(cross, first_inverse))
    zero = jnp.zeros((half, half), F32)
    pivot_factor = jnp.block([[first, zero], [cross, second]])
    pivot_inverse = jnp.block([[first_inverse, zero], [cross_inverse, second_inverse]])
    return (pivot_factor, pivot_inverse)


def split3(value):
    hi = value.astype(BF16)
    rest = value - hi.astype(F32)
    mid = rest.astype(BF16)
    return hi, mid, (rest - mid.astype(F32)).astype(BF16)


def dot_nt(a, b):
    return lax.dot_general(a, b, (((1,), (1,)), ((), ())), preferred_element_type=F32)


def spread_kernel(lane_start, src_ref, own_ref, far_ref, out_ref, *, window):
    ids = lax.broadcasted_iota(jnp.int32, (window, src_ref.shape[1]), 0)
    for child, ref in enumerate((own_ref, far_ref)):
        at = child * pl.num_programs(0) + pl.program_id(0)
        start = pl.multiple_of(lane_start[at] * 128, 128)
        pick = (ids == src_ref[child : child + 1, :] - start).astype(F32).astype(BF16)
        values = ref[:, pl.ds(start, window)]
        out_ref[0, child] = jnp.dot(values, pick, preferred_element_type=F32).astype(BF16)


def spread(own, far, lane_start, source_cols, grid_size, window):
    child_rows, child_order = own.shape
    rows_here = source_cols.shape[1] // grid_size
    return pl.pallas_call(
        functools.partial(spread_kernel, window=window),
        grid_spec=pltpu.PrefetchScalarGridSpec(
            num_scalar_prefetch=1,
            grid=(grid_size,),
            in_specs=[
                pl.BlockSpec((2, rows_here), lambda t, s: (0, t)),
                pl.BlockSpec((child_rows, child_order), lambda t, s: (0, 0)),
                pl.BlockSpec((child_rows, child_order), lambda t, s: (0, 0)),
            ],
            out_specs=pl.BlockSpec((1, 2, child_rows, rows_here), lambda t, s: (t, 0, 0, 0)),
        ),
        out_shape=jax.ShapeDtypeStruct((grid_size, 2, child_rows, rows_here), BF16),
        compiler_params=pltpu.CompilerParams(vmem_limit_bytes=VMEM_LIMIT),
        cost_estimate=pl.CostEstimate(
            flops=4 * child_rows * window * source_cols.shape[1],
            bytes_accessed=8 * child_rows * source_cols.shape[1],
            transcendentals=0,
        ),
    )(lane_start, source_cols, own, far)


def panels_kernel(inverse, c0, c1, c2, place, factors, solves, crosses, out_ref, parts, *, child_rows):
    tile = pl.program_id(0)
    per_device = child_rows // BLK
    units = TILE // BLK
    blocks = inverse.shape[0] // 2

    @pl.when(tile == 0)
    def _():
        for step in range(PANELS):
            for index, part in enumerate(split3(solves[step])):
                parts[step, index] = part

    rows = []
    for child in range(2):
        picked = []
        for chunk, pitch in ((c0, child_rows + EXTRA), (c1, child_rows), (c2, child_rows)):
            pieces = []
            for unit in range(units):
                block = inverse[child * blocks + tile * units + unit]
                safe = jnp.maximum(block, 0)
                at = (safe // per_device) * pitch + (safe % per_device) * BLK
                at = pl.multiple_of(at, 16)
                piece = chunk[pl.ds(at, BLK), child * PW : (child + 1) * PW].astype(F32)
                pieces.append(jnp.where(block >= 0, piece, 0.0).astype(BF16))
            picked.append(jnp.concatenate(pieces, axis=0))
        rows.append(picked)
    done = []
    for step in range(PANELS):
        low, high = step * PW, (step + 1) * PW
        total = jnp.zeros((TILE, PW), F32)
        for child in range(2):
            for chunk in range(step + 1):
                total += jnp.dot(
                    rows[child][chunk],
                    place[child, chunk * PW : (chunk + 1) * PW, low:high],
                    preferred_element_type=F32,
                )
        current = total.astype(BF16)
        for earlier in range(step):
            cross = crosses[low:high, earlier * PW : (earlier + 1) * PW]
            current = (current.astype(F32) - dot_nt(done[earlier], cross)).astype(BF16)
        solved = dot_nt(current, parts[step, 2]) + dot_nt(current, parts[step, 1])
        solved = solved + dot_nt(current, parts[step, 0])
        parts_of = []
        for part in range(TILE // PW):
            place_of = tile * (TILE // PW) + part
            value = solved[part * PW : (part + 1) * PW]
            value = jnp.where(place_of == step, factors[step], value)
            parts_of.append(jnp.where(place_of < step, 0.0, value).astype(BF16))
        chosen = jnp.concatenate(parts_of, axis=0)
        done.append(chosen)
        out_ref[:, low:high] = chosen


def panels(inverse, chunks, place, factors, solves, crosses, front_order, child_rows):
    whole = lambda shape: pl.BlockSpec(shape, lambda t, s: (0,) * len(shape))
    return pl.pallas_call(
        functools.partial(panels_kernel, child_rows=child_rows),
        grid_spec=pltpu.PrefetchScalarGridSpec(
            num_scalar_prefetch=1,
            grid=(front_order // TILE,),
            in_specs=[whole(x.shape) for x in (*chunks, place, factors, solves, crosses)],
            out_specs=pl.BlockSpec((TILE, TOP), lambda t, s: (t, 0)),
            scratch_shapes=[pltpu.VMEM((PANELS, 3, PW, PW), BF16)],
        ),
        out_shape=jax.ShapeDtypeStruct((front_order, TOP), BF16),
        compiler_params=pltpu.CompilerParams(vmem_limit_bytes=VMEM_LIMIT),
    )(inverse, *chunks, place, factors, solves, crosses)


def trailing_kernel(scalars, src_ref, diag_ref, rows_ref, mine_ref, tile_ref, out_ref, *, child_rows):
    tile = pl.program_id(0)
    rows_here = out_ref.shape[0]
    tiles = pl.num_programs(0)
    active, first_row = scalars[2 * tiles], scalars[2 * tiles + 1]

    @pl.when(tile < PANELS)
    def _():
        for step in range(PANELS):
            @pl.when(tile == step)
            def _():
                out_ref[...] = mine_ref[:, step * PW : (step + 1) * PW]

    @pl.when(tile >= PANELS)
    def _():
        ids = lax.broadcasted_iota(jnp.int32, (PW, PW), 0)
        total = None
        per_device = child_rows // BLK
        for child in range(2):
            first = scalars[child * tiles + tile]
            pick = (ids == src_ref[child : child + 1, :] - first * BLK).astype(F32).astype(BF16)
            pieces = []
            for unit in range(UNIT):
                block = first + unit
                at = ((block // per_device) * 2 + child) * child_rows + (block % per_device) * BLK
                pieces.append(rows_ref[pl.ds(pl.multiple_of(at, BLK), BLK), :])
            term = lax.dot_general(
                jnp.concatenate(pieces, axis=0), pick, (((0,), (0,)), ((), ())),
                preferred_element_type=F32,
            )
            total = term if total is None else total + term
        row = first_row + lax.broadcasted_iota(jnp.int32, (rows_here, PW), 0)
        col = tile * PW + lax.broadcasted_iota(jnp.int32, (rows_here, PW), 1)
        on_diag = row == col
        total = total + jnp.where(on_diag, diag_ref[...], 0.0)
        padding = (row >= active) | (col >= active)
        current = jnp.where(padding, jnp.where(on_diag, 1.0, 0.0), total).astype(BF16)
        for step in range(PANELS):
            low, high = step * PW, (step + 1) * PW
            product = dot_nt(mine_ref[:, low:high], tile_ref[:, low:high])
            current = (current.astype(F32) - product).astype(BF16)
        out_ref[...] = jnp.where(row < TOP, 0.0, current.astype(F32)).astype(BF16)


def trailing(scalars, source_rows, diag, rows, mine, factor, child_rows):
    front_order = factor.shape[0]
    rows_here = mine.shape[0]
    tiles = front_order // PW
    whole = lambda x: pl.BlockSpec(x.shape, lambda t, s: (0,) * x.ndim)
    return pl.pallas_call(
        functools.partial(trailing_kernel, child_rows=child_rows),
        grid_spec=pltpu.PrefetchScalarGridSpec(
            num_scalar_prefetch=1,
            grid=(tiles,),
            in_specs=[
                pl.BlockSpec((2, PW), lambda t, s: (0, t)),
                whole(diag), whole(rows), whole(mine),
                pl.BlockSpec((PW, TOP), lambda t, s: (t, 0)),
            ],
            out_specs=pl.BlockSpec((rows_here, PW), lambda t, s: (0, t)),
        ),
        out_shape=jax.ShapeDtypeStruct((rows_here, front_order), BF16),
        compiler_params=pltpu.CompilerParams(vmem_limit_bytes=VMEM_LIMIT),
    )(scalars, source_rows, diag, rows, mine, factor)


def pivot_chain(tops):
    factors, inverses, rows_of = [], [], []
    for step in range(PANELS):
        low = step * PW
        current = tops[step][low:]
        for earlier in range(step):
            lower = rows_of[earlier][low:]
            product = dot_nt(lower, lower[:PW])
            current = rounded(current - product)
        factor, inverse = pivot_parts(current[:PW])
        factors.append(factor)
        inverses.append(inverse)
        below = rounded(highest(current[PW:], inverse.T)).astype(BF16)
        head = jnp.zeros((low + PW, PW), BF16)
        rows_of.append(jnp.concatenate([head, below], axis=0))
    return jnp.stack(factors), jnp.stack(inverses), jnp.concatenate(rows_of, axis=1)


def body(front_diag, children, parent, front_blocks, child_blocks, row_map):
    leaf_id = lax.axis_index("leaf")
    grid_id = lax.axis_index("grid")
    grid_size = lax.axis_size("grid")
    rows_here = front_diag.shape[1]
    front_order = rows_here * grid_size
    child_rows = children.shape[1]
    child_order = children.shape[2]
    blocks_front = front_order // BLK
    blocks_child = child_order // BLK
    partner = jnp.bitwise_xor(leaf_id, 1)
    first_child = 2 * leaf_id
    keep_first = parent[first_child] == leaf_id
    own_child = jnp.where(keep_first, first_child, first_child + 1)
    partner_first = 2 * partner
    far_child = jnp.where(parent[partner_first] == leaf_id, partner_first, partner_first + 1)
    own_part = jnp.where(keep_first, children[0], children[1])
    away_part = jnp.where(keep_first, children[1], children[0])

    strip_far = swapped(away_part[:, :TOP], "leaf", 0)
    arrived = swapped(away_part, "leaf", 0)
    high_part = rounded(front_diag[0])
    mid_part = rounded(front_diag[0] - high_part)
    low_part = front_diag[0] - high_part - mid_part
    packed = jnp.concatenate([high_part, mid_part, low_part]).astype(BF16)
    packed = jnp.pad(packed, (0, EXTRA * 2 * PW - 3 * rows_here)).reshape(EXTRA, 2 * PW)
    chunks = []
    for step in range(PANELS):
        low, high = step * PW, (step + 1) * PW
        pair = jnp.concatenate([own_part[:, low:high], strip_far[:, low:high]], axis=1)
        if step == 0:
            pair = jnp.concatenate([pair, packed], axis=0)
        chunks.append(lax.all_gather(pair, "grid", axis=0, tiled=True))

    ids = jnp.stack([own_child, far_child])
    maps = row_map[ids]
    live = jnp.arange(blocks_child)[None, :] < child_blocks[ids][:, None]
    hits = (maps[:, :, None] == jnp.arange(blocks_front)[None, None, :]) & live[:, :, None]
    inverse = jnp.max(jnp.where(hits, jnp.arange(blocks_child)[None, :, None], -1), axis=1)
    source = jnp.where(
        inverse[:, :, None] >= 0, inverse[:, :, None] * BLK + jnp.arange(BLK), -(2**20)
    ).reshape(2, front_order).astype(jnp.int32)
    filled = (inverse >= 0).astype(jnp.int32)
    before = jnp.cumsum(filled, axis=1) - filled
    per_device = rows_here // BLK
    window = (per_device + 2) * BLK
    lane_start = jnp.minimum(before[:, ::per_device] // 2, (child_order - window) // 128)
    row_start = jnp.minimum(before[:, ::UNIT], blocks_child - UNIT)

    outgoing = spread(own_part, arrived, lane_start.reshape(-1), source, grid_size, window)
    incoming = lax.all_to_all(outgoing, "grid", split_axis=0, concat_axis=0, tiled=True)

    devices = -(-TOP // child_rows)
    first_chunk = chunks[0][: devices * (child_rows + EXTRA)]
    first_chunk = first_chunk.reshape(devices, child_rows + EXTRA, 2 * PW)[:, :child_rows]
    heads = [first_chunk.reshape(devices * child_rows, 2 * PW)[:TOP]]
    heads += [chunk[:TOP] for chunk in chunks[1:]]
    holders = -(-TOP // rows_here)
    carried = chunks[0][: holders * (child_rows + EXTRA)]
    carried = carried.reshape(holders, child_rows + EXTRA, 2 * PW)[:, child_rows:]
    carried = carried.reshape(holders, -1)[:, : 3 * rows_here].reshape(holders, 3, rows_here)
    carried = carried.astype(F32)
    diag_top = ((carried[:, 2] + carried[:, 1]) + carried[:, 0]).reshape(-1)[:TOP]

    place = (jnp.arange(TOP)[None, :, None] == source[:, None, :TOP]).astype(BF16)
    tops = []
    for step in range(PANELS):
        low, high = step * PW, (step + 1) * PW
        total = jnp.zeros((TOP, PW), F32)
        for child in range(2):
            part = jnp.zeros((TOP, PW), F32)
            for chunk in range(step + 1):
                rows = heads[chunk][:, child * PW : (child + 1) * PW]
                part = part + jnp.dot(
                    rows, place[child, chunk * PW : (chunk + 1) * PW, low:high],
                    preferred_element_type=F32,
                )
            total = total + lax.dot_general(
                place[child], part.astype(BF16), (((0,), (0,)), ((), ())),
                preferred_element_type=F32,
            )
        shifted = jnp.arange(TOP)[:, None] == jnp.arange(low, high)[None, :]
        total = total + jnp.where(shifted, diag_top[:, None], 0.0)
        tops.append(rounded(total))
    factors, inverses, crosses = pivot_chain(tops)
    factor = panels(
        inverse.reshape(-1).astype(jnp.int32), chunks, place, factors, inverses, crosses, front_order, child_rows
    )
    mine = lax.dynamic_slice_in_dim(factor, grid_id * rows_here, rows_here, axis=0)
    scalars = jnp.concatenate(
        [row_start.reshape(-1), (front_blocks[leaf_id] * BLK)[None], (grid_id * rows_here)[None]]
    ).astype(jnp.int32)
    matrix = trailing(
        scalars, source, front_diag[0][:, None],
        incoming.reshape(2 * child_order, rows_here), mine, factor, child_rows,
    )
    return matrix[None]


def solution(mesh):
    in_specs = (P("leaf", "grid"), P("leaf", "grid", None), P(), P(), P(), P())
    out_specs = P("leaf", "grid", None)
    return jax.shard_map(body, mesh=mesh, in_specs=in_specs, out_specs=out_specs, check_vma=False)
```
